32 devices in a mesh: lift: 4 (over z), tile: 8 (over y, x, core).
Axes of the slice: x: 2, y: 2, z: 4, core: 2. Of those that a mesh axis runs over, the one named last changes fastest.
Arguments:
- oxygen: float32 [4, 16, 8, 256, 256], P('lift', None, 'tile'), may hold values from 0 to 1
- velocity: float32 [4, 16, 8, 256, 256], P('lift', None, 'tile'), may hold values from 0.2 to 1
- spacing: float32 [4], P('lift'), may hold values from 1 to 2
- inlets: int32 [4, 8, 256, 256], P('lift', 'tile'), may hold values 0 or 1
- proj_x: float32 [4, 8, 4, 256, 256], P('lift', 'tile'), may hold values from -1 to 1
- proj_y: float32 [4, 8, 4, 256, 256], P('lift', 'tile'), may hold values from -1 to 1
- sources: int32 [4, 8, 4], P('lift', 'tile'), may hold values from 0 to 7, as said below
Outputs:
- oxygen_next: float32 [4, 16, 8, 256, 256], P('lift', None, 'tile')
The draws below stay inside these ranges and needn't reach their ends.
Inputs may be any that keep to these rules, and one draw needn't show every extreme that they name: sources[l, t, 0] is the tile (t + 4) % 8; the other entries may be any tile of the lift below; entries of lift 0 are not used.
All inputs are finite; a program needn't handle non-finite values. No bound on the sum of `inlets` on one device may be relied on, other than what follows from the above.
Results may differ from the reference program's by a relative error of at most 0.0001.
Values sent between devices are 32-bit elements; how exact they have to be, the bound alone decides.
A program may use at most 128 MiB of HBM per device.

```python
import math
import jax
import jax.numpy as jnp
from jax import lax

NZ = 16
CX = 256
CY = 256
TCOL = 4
K = 4
STEPS = 2
LIFTS = 4
TILES = 8


def projection_block(key, width):
    key_diag, key_off = jax.random.split(key)
    shape = (LIFTS, TILES, K, width, width)
    diagonal = jax.random.uniform(key_diag, shape, jnp.float32, 0.5, 1.0)
    off_part = jax.random.uniform(key_off, shape, jnp.float32, -1.0, 1.0) * (0.6 / math.sqrt(width))
    row_index = lax.broadcasted_iota(jnp.int32, shape, 3)
    col_index = lax.broadcasted_iota(jnp.int32, shape, 4)
    identity = (row_index == col_index).astype(jnp.float32)
    return (identity * diagonal + (1.0 - identity) * off_part) * K ** (-0.5)


def draw_proj_x(key, part):
    return projection_block(jax.random.fold_in(key, 11), CX)


def draw_proj_y(key, part):
    return projection_block(jax.random.fold_in(key, 23), CY)


def draw_sources(key, part):
    shape = (LIFTS, TILES, K)
    drawn = jax.random.randint(jax.random.fold_in(key, 37), shape, 0, TILES)
    tile_ids = lax.broadcasted_iota(jnp.int32, shape, 1)
    slot_ids = lax.broadcasted_iota(jnp.int32, shape, 2)
    partner = (tile_ids + TILES // 2) % TILES
    return jnp.where(slot_ids == 0, partner, drawn).astype(jnp.int32)


def with_ends(array, stream_key, smallest, largest):
    longest = array.shape.index(max(array.shape))
    spots = []
    for shift in (0, 1):
        where = [jax.random.randint(jax.random.fold_in(stream_key, axis), (), 0, length) for axis, length in enumerate(array.shape)]
        where[longest] = (where[longest] + shift) % array.shape[longest]
        spots.append(tuple(where))
    return array.at[spots[0]].set(smallest).at[spots[1]].set(largest)


def block_scale(own_key, shape, cuts, low, high):
    def one(axis_at, blocks):
        steps = jax.random.uniform(jax.random.fold_in(jax.random.fold_in(own_key, 6), axis_at), (blocks,), jnp.float32, low / len(cuts), high / len(cuts))
        return jnp.repeat(jnp.exp(steps), shape[axis_at] // blocks).reshape((-1,) + (1,) * (len(shape) - axis_at - 1))

    level = one(*cuts[0])
    for cut in cuts[1:]:
        level = level * one(*cut)
    return level


def setup_inputs(seed: int = 0) -> dict:
    splits = jax.random.split(jax.random.key(seed), 8)
    return {
        "oxygen": jnp.clip(1.0 * jax.random.uniform(splits[0], (LIFTS, NZ, TILES, CX, CY), jnp.float32) ** block_scale(splits[0], (LIFTS, NZ, TILES, CX, CY), ((0, 4), (2, 8)), -0.2, 0.2), 0.0, 1.0),
        "velocity": jnp.clip(0.2 + 0.8 * jax.random.uniform(splits[1], (LIFTS, NZ, TILES, CX, CY), jnp.float32) ** block_scale(splits[1], (LIFTS, NZ, TILES, CX, CY), ((0, 4), (2, 8)), -0.2, 0.2), 0.2, 1.0),
        "spacing": jnp.clip(jnp.exp(math.log(2.0) - 0.6931472 * jax.random.uniform(splits[2], (LIFTS,), jnp.float32) ** block_scale(splits[2], (LIFTS,), ((0, 4),), -0.2, 0.2)), 1.0, 2.0),
        "inlets": with_ends((jax.random.randint(splits[3], (LIFTS, TILES, CX, CY), 0, 8) < 1).astype(jnp.int32), jax.random.fold_in(splits[3], 1), 0, 1),
        "proj_x": draw_proj_x(jax.random.fold_in(splits[7], 71), 0),
        "proj_y": draw_proj_y(jax.random.fold_in(splits[7], 71), 0),
        "sources": draw_sources(jax.random.fold_in(splits[7], 71), 0),
    }


TIME_STEP = 0.1
INJECT_RATE = 2.0
AMBIENT = 1.0
HIGHEST = lax.Precision.HIGHEST


def horizontal(field):
    lifts, depth, tiles, width_x, width_y = field.shape
    tile_rows = tiles // TCOL
    grid = field.reshape(lifts, depth, tile_rows, TCOL, width_x, width_y)
    grid = grid.transpose(0, 1, 2, 4, 3, 5).reshape(lifts, depth, tile_rows * width_x, TCOL * width_y)
    padded = jnp.pad(grid, ((0, 0), (0, 0), (1, 1), (1, 1)))
    beside_all = padded[:, :, 2:, 1:-1] + padded[:, :, :-2, 1:-1] + padded[:, :, 1:-1, 2:] + padded[:, :, 1:-1, :-2]
    lapl = beside_all - 4.0 * grid
    lapl = lapl.reshape(lifts, depth, tile_rows, width_x, TCOL, width_y).transpose(0, 1, 2, 4, 3, 5)
    return lapl.reshape(field.shape)


def pick_planes(planes, index):
    return planes[index]


def reference(oxygen, velocity, spacing, inlets, proj_x, proj_y, sources):
    field = oxygen
    inverse = (1.0 / (spacing * spacing))[:, None, None, None, None]
    inject = INJECT_RATE * inlets.astype(jnp.float32)
    onehot = (sources[1:, :, :, None] == jnp.arange(TILES, dtype=jnp.int32)).astype(jnp.float32)
    for step_index in range(STEPS):
        top_plane = field[:, NZ - 1]
        bottom_plane = field[:, 0]
        picked = jax.vmap(pick_planes)(top_plane[:-1], sources[1:])
        from_below = jnp.einsum('ltkab,ltkbc,ltkdc->ltad', proj_x[1:], picked, proj_y[1:], precision=HIGHEST)
        ghost_below = jnp.concatenate([jnp.zeros((1, TILES, CX, CY), jnp.float32), from_below], axis=0)
        pieces = jnp.einsum('ltkba,ltbc,ltkcd->ltkad', proj_x[1:], bottom_plane[1:], proj_y[1:], precision=HIGHEST)
        from_above = jnp.einsum('ltks,ltkad->lsad', onehot, pieces, precision=HIGHEST)
        ghost_above = jnp.concatenate([from_above, jnp.full((1, TILES, CX, CY), AMBIENT, jnp.float32)], axis=0)
        stacked = jnp.concatenate([ghost_below[:, None], field, ghost_above[:, None]], axis=1)
        under = stacked[:, :-2]
        over = stacked[:, 2:]
        change = inverse * horizontal(field) + over + under - 2.0 * field - velocity * (field - under)
        change = change.at[:, 0].add(inject * (1.0 - field[:, 0]))
        field = field + TIME_STEP * change
    return field
```

```python
import functools

import jax
import jax.numpy as jnp
from jax import lax
from jax.experimental import pallas as pl
from jax.experimental.pallas import tpu as pltpu
from jax.sharding import PartitionSpec as P

TCOL = 4
STEPS = 2
TIME_STEP = 0.1
INJECT_RATE = 2.0
AMBIENT = 1.0
MESH = pl.DeviceIdType.MESH
CHUNKS = 4
STRIP = 32
LANES = 128
ALL, INNER, TOP, BOTTOM = 0, 1, 2, 3
F32 = jnp.float32
BF16 = jnp.bfloat16


def split(value):
    high = value.astype(BF16)
    return high, (value - high.astype(F32)).astype(BF16)


def left_cat(value):
    high, low = split(value)
    return jnp.concatenate([high, low, high], axis=1)


def right_cat(value):
    high, low = split(value)
    return jnp.concatenate([high, high, low], axis=0)


def dot(left, right):
    return jnp.dot(left, right, preferred_element_type=F32)


def kernel(
    tiles, lifts, nb,
    sources_ref, spacing_ref, oxygen, velocity, inlets, proj_x, proj_y, out,
    f0, f1, f2, vel, inl, xw, yw,
    x_cat, xt_cat, y_cat, yt_cat, halves, pieces,
    tops_0, tops_1, acc, core_in, above_in, send_down, gbelow,
    hs, hr, hcol,
    load_sems, out_sems, halo_ss, halo_rs,
    ag_ss, ag_rs, rs_ss, rs_rs, z_ss, z_rs, hcol_in, *stage_in
):
    depth, cx, cy = f0.shape
    kk = xw.shape[0]
    rows = cx // CHUNKS
    tops = (tops_0, tops_1)
    tile = lax.axis_index("tile")
    lift = lax.axis_index("lift")
    column = tile % TCOL
    base = tile - column
    row_down = (tile + TCOL) % tiles
    row_up = (tile + tiles - TCOL) % tiles
    col_right = base + (column + 1) % TCOL
    col_left = base + (column + TCOL - 1) % TCOL
    has_above = lift < lifts - 1
    has_below = lift > 0

    def flipped(bit):
        size = 1 << bit
        return tile + size * (1 - 2 * ((tile // size) % 2))

    partner_core = flipped(0)
    partner = [flipped(nb - axis) for axis in range(nb)]

    bottom_load = pltpu.make_async_copy(oxygen.at[0], f0.at[0], load_sems.at[0])
    x_load = pltpu.make_async_copy(proj_x, xw, load_sems.at[1])
    y_load = pltpu.make_async_copy(proj_y, yw, load_sems.at[2])
    f_load = pltpu.make_async_copy(oxygen.at[pl.ds(1, depth - 1)], f0.at[pl.ds(1, depth - 1)], load_sems.at[3])
    v_load = pltpu.make_async_copy(velocity, vel, load_sems.at[4])
    i_load = pltpu.make_async_copy(inlets, inl, load_sems.at[5])
    for load in (bottom_load, x_load, y_load, f_load, v_load, i_load):
        load.start()

    barrier = pltpu.get_barrier_semaphore()
    peers = [partner_core] + partner + [row_down, row_up, col_right, col_left]
    for peer in peers:
        pl.semaphore_signal(barrier, inc=1, device_id={"tile": peer}, device_id_type=MESH)

    @pl.when(has_above)
    def _():
        pl.semaphore_signal(barrier, inc=1, device_id={"lift": lift + 1}, device_id_type=MESH)

    @pl.when(has_below)
    def _():
        pl.semaphore_signal(barrier, inc=1, device_id={"lift": lift - 1}, device_id_type=MESH)

    pl.semaphore_wait(barrier, len(peers) + has_above.astype(jnp.int32) + has_below.astype(jnp.int32))

    def cut(c):
        return pl.ds(c * rows, rows)

    def order(c):
        axes = list(range(nb))
        return axes if c % 2 == 0 else axes[::-1]

    def remote(src, dst, ss, rs, **where):
        return pltpu.make_async_remote_copy(
            src_ref=src, dst_ref=dst, send_sem=ss, recv_sem=rs, device_id=where, device_id_type=MESH
        )

    def top_up(s, c):
        field = oxygen if s == 0 else f1
        return remote(
            field.at[depth - 1, cut(c)],
            tops[s].at[(0,) + (0,) * nb + (cut(c),)],
            z_ss.at[s, 0, c], z_rs.at[s, 0, c], lift=lift + 1,
        )

    def spread(s, c, stage):
        if stage == nb:
            every = (slice(None),) * nb
            return remote(
                tops[s].at[(0,) + every + (cut(c),)], tops[s].at[(1,) + every + (cut(c),)],
                ag_ss.at[s, stage, c], ag_rs.at[s, stage, c], tile=partner_core,
            )
        axes = order(c)
        index = [0] * nb
        for axis in axes[:stage]:
            index[axis] = slice(None)
        there = list(index)
        there[axes[stage]] = 1
        return remote(
            tops[s].at[(0,) + tuple(index) + (cut(c),)], tops[s].at[(0,) + tuple(there) + (cut(c),)],
            ag_ss.at[s, stage, c], ag_rs.at[s, stage, c], tile=partner[axes[stage]],
        )

    def top_arrived(s, c):
        @pl.when(has_below)
        def _():
            top_up(s, c).wait_recv()

        @pl.when(lift == 0)
        def _():
            tops[s][(0,) + (0,) * nb + (cut(c),)] = jnp.zeros((rows, cy), F32)

    def reduce_core(s, c):
        every = (slice(None),) * nb
        return remote(
            acc.at[(s, 1) + every + (cut(c),)], core_in.at[(s,) + every + (cut(c),)],
            rs_ss.at[s, nb, c], rs_rs.at[s, nb, c], tile=partner_core,
        )

    def left_index(c, stage):
        axes = order(c)
        index = [slice(None)] * nb
        for axis in axes[:stage]:
            index[axis] = 0
        return index

    def reduce_stage(s, c, stage):
        axis = order(c)[stage]
        index = left_index(c, stage)
        index[axis] = 1
        every = (slice(None),) * (nb - 1 - stage)
        return remote(
            acc.at[(s, 0) + tuple(index) + (cut(c),)], stage_in[stage].at[(s,) + every + (cut(c),)],
            rs_ss.at[s, stage, c], rs_rs.at[s, stage, c], tile=partner[axis],
        )

    def add_core(s, c):
        reduce_core(s, c).wait_recv()
        every = (slice(None),) * nb
        at = (s, 0) + every + (cut(c),)
        acc[at] = acc[at] + core_in[(s,) + every + (cut(c),)]

    def add_stage(s, c, stage):
        reduce_stage(s, c, stage).wait_recv()
        index = tuple(left_index(c, stage + 1))
        at = (s, 0) + index + (cut(c),)
        every = (slice(None),) * (nb - 1 - stage)
        total = acc[at] + stage_in[stage][(s,) + every + (cut(c),)]
        if stage == nb - 1:
            send_down[s, cut(c)] = total
        else:
            acc[at] = total

    def sum_down(s, c):
        return remote(
            send_down.at[s, cut(c)], above_in.at[s, cut(c)],
            z_ss.at[s, 1, c], z_rs.at[s, 1, c], lift=lift - 1,
        )

    def ghost_above(s, c):
        @pl.when(has_above)
        def _():
            sum_down(s, c).wait_recv()

        @pl.when(lift == lifts - 1)
        def _():
            above_in[s, cut(c)] = jnp.full((rows, cy), AMBIENT, F32)

        return above_in[s, cut(c)]

    def if_below(copy_of, s, c, action):
        @pl.when(has_below)
        def _():
            getattr(copy_of(s, c), action)()

    def if_above(copy_of, s, c, action):
        @pl.when(has_above)
        def _():
            getattr(copy_of(s, c), action)()

    for c in range(CHUNKS):
        if_above(top_up, 0, c, "start")

    lane = lax.broadcasted_iota(jnp.int32, (STRIP, LANES), 1)
    halo_to = [row_down, row_up, col_right, col_left]

    def halo_copy(g, d):
        return remote(hs.at[g, d], hr.at[g, d], halo_ss.at[g, d], halo_rs.at[g, d], tile=halo_to[d])

    def halo_send(src, g, first, end):
        for z in range(first, end):
            hs[g, 0, z:z + 1, :] = src[z, cx - 1:cx, :]
            hs[g, 1, z:z + 1, :] = src[z, 0:1, :]

        def one(i, carry):
            at = pl.ds(pl.multiple_of(i * STRIP, STRIP), STRIP)
            right = jnp.zeros((STRIP, LANES), F32)
            left = jnp.zeros((STRIP, LANES), F32)
            for z in range(first, end):
                right = jnp.where(lane == z, pltpu.roll(src[z, at, cy - LANES:], (z + 1) % LANES, 1), right)
                rim = src[z, at, :LANES]
                left = jnp.where(lane == z, pltpu.roll(rim, z, 1) if z else rim, left)
            hcol[0, at] = right
            hcol[1, at] = left
            return carry

        lax.fori_loop(0, cx // STRIP, one, 0)
        hs[g, 2] = hcol[0].T[:depth]
        hs[g, 3] = hcol[1].T[:depth]
        for d in range(4):
            halo_copy(g, d).start()

    at_edge = [base == 0, base == tiles - TCOL, column == 0, column == TCOL - 1]

    def halo_receive(g):
        for d in range(4):
            halo_copy(g, d).wait_recv()
        for d in range(2):
            hr[g, d] = jnp.where(at_edge[d], 0.0, hr[g, d])
        for d in (2, 3):
            value = jnp.where(at_edge[d], 0.0, hr[g, d])
            padded = jnp.concatenate([value, jnp.zeros((LANES - depth, cx), F32)], axis=0)
            hcol_in[g, d - 2] = padded.T


    inverse = 1.0 / (spacing_ref[0] * spacing_ref[0])
    row_at = lax.broadcasted_iota(jnp.int32, (STRIP, cy), 0)
    strips = range(0, cx, STRIP)

    def stencil(src, z, g, r, under, over):
        at = pl.ds(r, STRIP)
        here = src[z, at]
        before = hr[g, 0, pl.ds(z, 1), :] if r == 0 else src[z, pl.ds(r - 1, 1), :]
        after = hr[g, 1, pl.ds(z, 1), :] if r == cx - STRIP else src[z, pl.ds(r + STRIP, 1), :]
        north = jnp.where(row_at == 0, before, pltpu.roll(here, 1, 0))
        south = jnp.where(row_at == STRIP - 1, after, pltpu.roll(here, STRIP - 1, 0))
        west = pltpu.roll(here, 1, 1)
        east = pltpu.roll(here, cy - 1, 1)
        west_rim = pltpu.roll(hcol_in[g, 0, at], (LANES - z) % LANES, 1)
        east_rim = pltpu.roll(hcol_in[g, 1, at], LANES - 1 - z, 1)
        west = jnp.concatenate([jnp.where(lane == 0, west_rim, west[:, :LANES]), west[:, LANES:]], axis=1)
        east = jnp.concatenate(
            [east[:, : cy - LANES], jnp.where(lane == LANES - 1, east_rim, east[:, cy - LANES:])], axis=1
        )
        change = (north + south + west + east - 4.0 * here) * inverse - 2.0 * here
        speed = vel[z, at]
        if under is None:
            change = change - speed * here
        else:
            below = src[under, at]
            change = change + below - speed * (here - below)
        if over is not None:
            change = change + src[over, at]
        return here, change

    def inner(src, dst, g, first, end):
        def one(z, carry):
            for r in strips:
                here, change = stencil(src, z, g, r, z - 1, z + 1)
                dst[z, pl.ds(r, STRIP)] = here + TIME_STEP * change
            return carry

        lax.fori_loop(first, end, one, 0)

    def top_part(src, dst, g):
        for r in strips:
            here, change = stencil(src, depth - 1, g, r, depth - 2, None)
            dst[depth - 1, pl.ds(r, STRIP)] = here + TIME_STEP * change

    def bottom_part(src, dst, g):
        for r in strips:
            at = pl.ds(r, STRIP)
            here, change = stencil(src, 0, g, r, None, 1)
            change = change + INJECT_RATE * inl[at].astype(F32) * (1.0 - here)
            dst[0, at] = here + TIME_STEP * change

    def top_add(s, dst, c):
        dst[depth - 1, cut(c)] = dst[depth - 1, cut(c)] + TIME_STEP * ghost_above(s, c)

    def bottom_add(s, dst):
        for r in strips:
            at = pl.ds(r, STRIP)
            ghost = jnp.where(has_below, gbelow[at], 0.0)
            dst[0, at] = dst[0, at] + TIME_STEP * ((1.0 + vel[0, at]) * ghost)

    def prepare_down():
        x_load.wait()
        y_load.wait()
        for k in range(kk):
            xt_cat[pl.ds(k * cx, cx)] = left_cat(xw[k].T)
            y_cat[k] = right_cat(yw[k])

    def prepare_up():
        for k in range(kk):
            x_cat[k] = left_cat(xw[k])
            yt_cat[pl.ds(3 * k * cy, 3 * cy)] = right_cat(yw[k].T)

    def project_down(plane):
        field = right_cat(plane)
        for k in range(kk):
            half = left_cat(dot(xt_cat[pl.ds(k * cx, cx)], field))
            pieces[k] = dot(half, y_cat[k])

    size_of = [1] + [1 << (nb - axis) for axis in range(nb)]

    def slot_tile(bits):
        there = tile
        for bit, size in zip(bits, size_of):
            if bit:
                there = there + size * (1 - 2 * ((tile // size) % 2))
        return there

    all_slots = [[slot % 2] + [(slot >> (nb - axis)) % 2 for axis in range(nb)] for slot in range(tiles)]
    listed = [sources_ref[0, 0, k] for k in range(kk)]
    wanted = [[listed[k] == slot_tile(bits) for k in range(kk)] for bits in all_slots]

    def fill(s, c):
        for r in range(0, rows, STRIP):
            at = pl.ds(c * rows + r, STRIP)
            values = [pieces[k, at] for k in range(kk)]
            for slot, bits in enumerate(all_slots):
                total = values[0] if slot == tiles // 2 else None
                for k in range(1, kk):
                    term = jnp.where(wanted[slot][k], values[k], 0.0)
                    total = term if total is None else total + term
                acc[(s,) + tuple(bits) + (at,)] = total

    def project_up(s):
        for k in range(kk):
            at = tuple((listed[k] // size + tile // size) % 2 for size in size_of)
            half = dot(x_cat[k], right_cat(tops[s][at]))
            halves[:, pl.ds(3 * k * cy, 3 * cy)] = left_cat(half)
        gbelow[...] = dot(halves[...], yt_cat[...])

    def put(z0, n, i):
        return pltpu.make_async_copy(f2.at[pl.ds(z0, n)], out.at[pl.ds(z0, n)], out_sems.at[i])

    def reduce_pipeline(s, between):
        for turn in range(CHUNKS + nb + 1):
            if turn < CHUNKS:
                fill(s, turn)
                reduce_core(s, turn).start()
            c = turn - 1
            if 0 <= c < CHUNKS:
                add_core(s, c)
                reduce_stage(s, c, 0).start()
            for stage in range(nb):
                c = turn - 2 - stage
                if 0 <= c < CHUNKS:
                    add_stage(s, c, stage)
                    if stage == nb - 1:
                        if_below(sum_down, s, c, "start")
                    else:
                        reduce_stage(s, c, stage + 1).start()
            between(turn)

    def spread_turn(s, turn):
        c = turn
        if 0 <= c < CHUNKS:
            top_arrived(s, c)
            spread(s, c, 0).start()
        for stage in range(nb + 1):
            c = turn - 1 - stage
            if 0 <= c < CHUNKS:
                spread(s, c, stage).wait_recv()
                if stage < nb:
                    spread(s, c, stage + 1).start()

    spread_turns = CHUNKS + nb + 1

    prepare_down()
    bottom_load.wait()
    project_down(f0[0])

    hs[...] = jnp.zeros_like(hs)

    def between_first(turn):
        if turn >= CHUNKS:
            spread_turn(0, turn - CHUNKS)
        if turn == 0:
            f_load.wait()
            halo_send(f0, ALL, 0, depth)
        if turn == 1:
            prepare_up()
        if turn == 3:
            v_load.wait()
            i_load.wait()
            halo_receive(ALL)
            top_part(f0, f1, ALL)
        if turn == 4:
            bottom_part(f0, f1, ALL)
        if turn == 5:
            inner(f0, f1, ALL, 1, 3)

    reduce_pipeline(0, between_first)

    for turn in range(CHUNKS):
        spread_turn(0, turn + nb + 1)
        top_add(0, f1, turn)
        if_above(top_up, 1, turn, "start")
        inner(f0, f1, ALL, 3 + 3 * turn, 6 + 3 * turn)

    spread_turn(1, 0)
    spread_turn(1, 1)
    project_up(0)
    bottom_add(0, f1)
    spread_turn(1, 2)
    project_down(f1[0])
    spread_turn(1, 3)
    halo_send(f1, INNER, 1, depth - 1)
    halo_send(f1, TOP, depth - 1, depth)
    halo_send(f1, BOTTOM, 0, 1)
    spread_turn(1, 4)

    def between_second(turn):
        if 5 + turn < spread_turns:
            spread_turn(1, 5 + turn)
        if turn == 2:
            halo_receive(INNER)
            inner(f1, f2, INNER, 1, 5)
        if turn == 3:
            project_up(1)
            halo_receive(BOTTOM)
            bottom_part(f1, f2, BOTTOM)
            bottom_add(1, f2)
        if turn == 4:
            halo_receive(TOP)
            top_part(f1, f2, TOP)
            inner(f1, f2, INNER, 5, 8)
            put(0, 8, 0).start()
        if turn == 5:
            inner(f1, f2, INNER, 8, 12)
        if turn == 6:
            inner(f1, f2, INNER, 12, depth - 1)
            put(8, depth - 9, 1).start()

    reduce_pipeline(1, between_second)
    for c in range(CHUNKS):
        top_add(1, f2, c)
    put(depth - 1, 1, 2).start()

    for s in range(STEPS):
        for c in range(CHUNKS):
            if_above(top_up, s, c, "wait_send")
            if_below(sum_down, s, c, "wait_send")
            reduce_core(s, c).wait_send()
            for stage in range(nb):
                reduce_stage(s, c, stage).wait_send()
            for stage in range(nb + 1):
                spread(s, c, stage).wait_send()
    for g in range(4):
        for d in range(4):
            halo_copy(g, d).wait_send()
    put(0, 8, 0).wait()
    put(8, depth - 9, 1).wait()
    put(depth - 1, 1, 2).wait()


def on_device(tiles, lifts, oxygen, velocity, spacing, inlets, proj_x, proj_y, sources):
    nb = tiles.bit_length() - 2
    field = oxygen[0, :, 0]
    speed = velocity[0, :, 0]
    depth, cx, cy = field.shape
    kk = proj_x.shape[2]
    two = (2,) * nb
    any_spec = pl.BlockSpec(memory_space=pl.ANY)
    smem = pl.BlockSpec(memory_space=pltpu.SMEM)
    plane = (cx, cy)
    dma = pltpu.SemaphoreType.DMA
    result = pl.pallas_call(
        functools.partial(kernel, tiles, lifts, nb),
        out_shape=jax.ShapeDtypeStruct(field.shape, F32),
        in_specs=[smem, smem] + [any_spec] * 5,
        out_specs=any_spec,
        scratch_shapes=[
            pltpu.VMEM(field.shape, F32),
            pltpu.VMEM(field.shape, F32),
            pltpu.VMEM(field.shape, F32),
            pltpu.VMEM(field.shape, F32),
            pltpu.VMEM(plane, jnp.int32),
            pltpu.VMEM((kk,) + plane, F32),
            pltpu.VMEM((kk,) + plane, F32),
        ]
        + [
            pltpu.VMEM((kk, cx, 3 * cx), BF16),
            pltpu.VMEM((kk * cx, 3 * cx), BF16),
            pltpu.VMEM((kk, 3 * cy, cy), BF16),
            pltpu.VMEM((3 * kk * cy, cy), BF16),
            pltpu.VMEM((cx, 3 * kk * cy), BF16),
            pltpu.VMEM((kk,) + plane, F32),
            pltpu.VMEM((2,) + two + plane, F32),
            pltpu.VMEM((2,) + two + plane, F32),
            pltpu.VMEM((STEPS, 2) + two + plane, F32),
            pltpu.VMEM((STEPS,) + two + plane, F32),
            pltpu.VMEM((STEPS,) + plane, F32),
            pltpu.VMEM((STEPS,) + plane, F32),
            pltpu.VMEM(plane, F32),
            pltpu.VMEM((4, 4, depth, cx), F32),
            pltpu.VMEM((4, 4, depth, cx), F32),
            pltpu.VMEM((2, cx, LANES), F32),
            dma((6,)),
            dma((3,)),
            dma((4, 4)),
            dma((4, 4)),
            dma((STEPS, nb + 1, CHUNKS)),
            dma((STEPS, nb + 1, CHUNKS)),
            dma((STEPS, nb + 1, CHUNKS)),
            dma((STEPS, nb + 1, CHUNKS)),
            dma((STEPS, 2, CHUNKS)),
            dma((STEPS, 2, CHUNKS)),
            pltpu.VMEM((4, 2, cx, LANES), F32),
        ]
        + [pltpu.VMEM((STEPS,) + (2,) * (nb - 1 - stage) + plane, F32) for stage in range(nb)],
        compiler_params=pltpu.CompilerParams(
            collective_id=0, has_side_effects=True, vmem_limit_bytes=60 * 1024 * 1024
        ),
        cost_estimate=pl.CostEstimate(flops=10**9, bytes_accessed=16 * 1024 * 1024, transcendentals=0),
    )(sources, spacing, field, speed, inlets[0, 0], proj_x[0, 0], proj_y[0, 0])
    return result[None, :, None]


def solution(mesh):
    return jax.shard_map(
        functools.partial(on_device, mesh.shape["tile"], mesh.shape["lift"]),
        mesh=mesh,
        in_specs=(
            P("lift", None, "tile", None, None),
            P("lift", None, "tile", None, None),
            P("lift"),
            P("lift", "tile", None, None),
            P("lift", "tile", None, None, None),
            P("lift", "tile", None, None, None),
            P("lift", "tile", None),
        ),
        out_specs=P("lift", None, "tile", None, None),
        check_vma=False,
    )
```

```python
import functools

import jax
import jax.numpy as jnp
from jax import lax
from jax.experimental import pallas as pl
from jax.experimental.pallas import tpu as pltpu
from jax.sharding import PartitionSpec as P

TCOL = 4
STEPS = 2
TIME_STEP = 0.1
INJECT_RATE = 2.0
AMBIENT = 1.0
MESH = pl.DeviceIdType.MESH
CHUNKS = 4
STRIP = 32
LANES = 128
ALL, INNER, TOP, BOTTOM = 0, 1, 2, 3
F32 = jnp.float32
BF16 = jnp.bfloat16


def split(value):
    high = value.astype(BF16)
    return high, (value - high.astype(F32)).astype(BF16)


def left_cat(value):
    high, low = split(value)
    return jnp.concatenate([high, low, high], axis=1)


def right_cat(value):
    high, low = split(value)
    return jnp.concatenate([high, high, low], axis=0)


def dot(left, right):
    return jnp.dot(left, right, preferred_element_type=F32)


def kernel(
    tiles, lifts, nb,
    sources_ref, spacing_ref, oxygen, velocity, inlets, proj_x, proj_y, out,
    f0, f1, f2, vel, inl, xw, yw,
    x_cat, xt_cat, y_cat, yt_cat, halves, pieces,
    tops_0, tops_1, acc, core_in, above_in, send_down, gbelow,
    hs, hr, hcol,
    load_sems, out_sems, halo_ss, halo_rs,
    ag_ss, ag_rs, rs_ss, rs_rs, z_ss, z_rs, hcol_in, *stage_in
):
    depth, cx, cy = f0.shape
    kk = xw.shape[0]
    rows = cx // CHUNKS
    tops = (tops_0, tops_1)
    tile = lax.axis_index("tile")
    lift = lax.axis_index("lift")
    column = tile % TCOL
    base = tile - column
    row_down = (tile + TCOL) % tiles
    row_up = (tile + tiles - TCOL) % tiles
    col_right = base + (column + 1) % TCOL
    col_left = base + (column + TCOL - 1) % TCOL
    has_above = lift < lifts - 1
    has_below = lift > 0

    def flipped(bit):
        size = 1 << bit
        return tile + size * (1 - 2 * ((tile // size) % 2))

    partner_core = flipped(0)
    partner = [flipped(nb - axis) for axis in range(nb)]

    bottom_load = pltpu.make_async_copy(oxygen.at[0], f0.at[0], load_sems.at[0])
    x_load = pltpu.make_async_copy(proj_x, xw, load_sems.at[1])
    y_load = pltpu.make_async_copy(proj_y, yw, load_sems.at[2])
    f_load = pltpu.make_async_copy(oxygen.at[pl.ds(1, depth - 1)], f0.at[pl.ds(1, depth - 1)], load_sems.at[3])
    v_load = pltpu.make_async_copy(velocity, vel, load_sems.at[4])
    i_load = pltpu.make_async_copy(inlets, inl, load_sems.at[5])
    for load in (bottom_load, x_load, y_load, f_load, v_load, i_load):
        load.start()

    barrier = pltpu.get_barrier_semaphore()
    peers = [partner_core] + partner + [row_down, row_up, col_right, col_left]
    for peer in peers:
        pl.semaphore_signal(barrier, inc=1, device_id={"tile": peer}, device_id_type=MESH)

    @pl.when(has_above)
    def _():
        pl.semaphore_signal(barrier, inc=1, device_id={"lift": lift + 1}, device_id_type=MESH)

    @pl.when(has_below)
    def _():
        pl.semaphore_signal(barrier, inc=1, device_id={"lift": lift - 1}, device_id_type=MESH)

    pl.semaphore_wait(barrier, len(peers) + has_above.astype(jnp.int32) + has_below.astype(jnp.int32))

    def cut(c):
        return pl.ds(c * rows, rows)

    def order(c):
        axes = list(range(nb))
        return axes if c % 2 == 0 else axes[::-1]

    def remote(src, dst, ss, rs, **where):
        return pltpu.make_async_remote_copy(
            src_ref=src, dst_ref=dst, send_sem=ss, recv_sem=rs, device_id=where, device_id_type=MESH
        )

    def top_up(s, c):
        field = oxygen if s == 0 else f1
        return remote(
            field.at[depth - 1, cut(c)],
            tops[s].at[(0,) + (0,) * nb + (cut(c),)],
            z_ss.at[s, 0, c], z_rs.at[s, 0, c], lift=lift + 1,
        )

    def spread(s, c, stage):
        if stage == nb:
            every = (slice(None),) * nb
            return remote(
                tops[s].at[(0,) + every + (cut(c),)], tops[s].at[(1,) + every + (cut(c),)],
                ag_ss.at[s, stage, c], ag_rs.at[s, stage, c], tile=partner_core,
            )
        axes = order(c)
        index = [0] * nb
        for axis in axes[:stage]:
            index[axis] = slice(None)
        there = list(index)
        there[axes[stage]] = 1
        return remote(
            tops[s].at[(0,) + tuple(index) + (cut(c),)], tops[s].at[(0,) + tuple(there) + (cut(c),)],
            ag_ss.at[s, stage, c], ag_rs.at[s, stage, c], tile=partner[axes[stage]],
        )

    def top_arrived(s, c):
        @pl.when(has_below)
        def _():
            top_up(s, c).wait_recv()

        @pl.when(lift == 0)
        def _():
            tops[s][(0,) + (0,) * nb + (cut(c),)] = jnp.zeros((rows, cy), F32)

    def reduce_core(s, c):
        every = (slice(None),) * nb
        return remote(
            acc.at[(s, 1) + every + (cut(c),)], core_in.at[(s,) + every + (cut(c),)],
            rs_ss.at[s, nb, c], rs_rs.at[s, nb, c], tile=partner_core,
        )

    def left_index(c, stage):
        axes = order(c)
        index = [slice(None)] * nb
        for axis in axes[:stage]:
            index[axis] = 0
        return index

    def reduce_stage(s, c, stage):
        axis = order(c)[stage]
        index = left_index(c, stage)
        index[axis] = 1
        every = (slice(None),) * (nb - 1 - stage)
        return remote(
            acc.at[(s, 0) + tuple(index) + (cut(c),)], stage_in[stage].at[(s,) + every + (cut(c),)],
            rs_ss.at[s, stage, c], rs_rs.at[s, stage, c], tile=partner[axis],
        )

    def add_core(s, c):
        reduce_core(s, c).wait_recv()
        every = (slice(None),) * nb
        at = (s, 0) + every + (cut(c),)
        acc[at] = acc[at] + core_in[(s,) + every + (cut(c),)]

    def add_stage(s, c, stage):
        reduce_stage(s, c, stage).wait_recv()
        index = tuple(left_index(c, stage + 1))
        at = (s, 0) + index + (cut(c),)
        every = (slice(None),) * (nb - 1 - stage)
        total = acc[at] + stage_in[stage][(s,) + every + (cut(c),)]
        if stage == nb - 1:
            send_down[s, cut(c)] = total
        else:
            acc[at] = total

    def sum_down(s, c):
        return remote(
            send_down.at[s, cut(c)], above_in.at[s, cut(c)],
            z_ss.at[s, 1, c], z_rs.at[s, 1, c], lift=lift - 1,
        )

    def ghost_above(s, c):
        @pl.when(has_above)
        def _():
            sum_down(s, c).wait_recv()

        @pl.when(lift == lifts - 1)
        def _():
            above_in[s, cut(c)] = jnp.full((rows, cy), AMBIENT, F32)

        return above_in[s, cut(c)]

    def if_below(copy_of, s, c, action):
        @pl.when(has_below)
        def _():
            getattr(copy_of(s, c), action)()

    def if_above(copy_of, s, c, action):
        @pl.when(has_above)
        def _():
            getattr(copy_of(s, c), action)()

    for c in range(CHUNKS):
        if_above(top_up, 0, c, "start")

    lane = lax.broadcasted_iota(jnp.int32, (STRIP, LANES), 1)
    halo_to = [row_down, row_up, col_right, col_left]

    def halo_copy(g, d):
        return remote(hs.at[g, d], hr.at[g, d], halo_ss.at[g, d], halo_rs.at[g, d], tile=halo_to[d])

    def halo_send(src, g, first, end):
        for z in range(first, end):
            hs[g, 0, z:z + 1, :] = src[z, cx - 1:cx, :]
            hs[g, 1, z:z + 1, :] = src[z, 0:1, :]

        def one(i, carry):
            at = pl.ds(pl.multiple_of(i * STRIP, STRIP), STRIP)
            right = jnp.zeros((STRIP, LANES), F32)
            left = jnp.zeros((STRIP, LANES), F32)
            for z in range(first, end):
                right = jnp.where(lane == z, pltpu.roll(src[z, at, cy - LANES:], (z + 1) % LANES, 1), right)
                rim = src[z, at, :LANES]
                left = jnp.where(lane == z, pltpu.roll(rim, z, 1) if z else rim, left)
            hcol[0, at] = right
            hcol[1, at] = left
            return carry

        lax.fori_loop(0, cx // STRIP, one, 0)
        hs[g, 2] = hcol[0].T[:depth]
        hs[g, 3] = hcol[1].T[:depth]
        for d in range(4):
            halo_copy(g, d).start()

    at_edge = [base == 0, base == tiles - TCOL, column == 0, column == TCOL - 1]

    def halo_receive(g):
        for d in range(4):
            halo_copy(g, d).wait_recv()
        for d in range(2):
            hr[g, d] = jnp.where(at_edge[d], 0.0, hr[g, d])
        for d in (2, 3):
            value = jnp.where(at_edge[d], 0.0, hr[g, d])
            padded = jnp.concatenate([value, jnp.zeros((LANES - depth, cx), F32)], axis=0)
            hcol_in[g, d - 2] = padded.T


    inverse = 1.0 / (spacing_ref[0] * spacing_ref[0])
    row_at = lax.broadcasted_iota(jnp.int32, (STRIP, cy), 0)
    strips = range(0, cx, STRIP)

    def stencil(src, z, g, r, under, over):
        at = pl.ds(r, STRIP)
        here = src[z, at]
        before = hr[g, 0, pl.ds(z, 1), :] if r == 0 else src[z, pl.ds(r - 1, 1), :]
        after = hr[g, 1, pl.ds(z, 1), :] if r == cx - STRIP else src[z, pl.ds(r + STRIP, 1), :]
        north = jnp.where(row_at == 0, before, pltpu.roll(here, 1, 0))
        south = jnp.where(row_at == STRIP - 1, after, pltpu.roll(here, STRIP - 1, 0))
        west = pltpu.roll(here, 1, 1)
        east = pltpu.roll(here, cy - 1, 1)
        west_rim = pltpu.roll(hcol_in[g, 0, at], (LANES - z) % LANES, 1)
        east_rim = pltpu.roll(hcol_in[g, 1, at], LANES - 1 - z, 1)
        west = jnp.concatenate([jnp.where(lane == 0, west_rim, west[:, :LANES]), west[:, LANES:]], axis=1)
        east = jnp.concatenate(
            [east[:, : cy - LANES], jnp.where(lane == LANES - 1, east_rim, east[:, cy - LANES:])], axis=1
        )
        change = (north + south + west + east - 4.0 * here) * inverse - 2.0 * here
        speed = vel[z, at]
        if under is None:
            change = change - speed * here
        else:
            below = src[under, at]
            change = change + below - speed * (here - below)
        if over is not None:
            change = change + src[over, at]
        return here, change

    def inner(src, dst, g, first, end):
        def one(z, carry):
            for r in strips:
                here, change = stencil(src, z, g, r, z - 1, z + 1)
                dst[z, pl.ds(r, STRIP)] = here + TIME_STEP * change
            return carry

        lax.fori_loop(first, end, one, 0)

    def top_part(src, dst, g):
        for r in strips:
            here, change = stencil(src, depth - 1, g, r, depth - 2, None)
            dst[depth - 1, pl.ds(r, STRIP)] = here + TIME_STEP * change

    def bottom_part(src, dst, g):
        for r in strips:
            at = pl.ds(r, STRIP)
            here, change = stencil(src, 0, g, r, None, 1)
            change = change + INJECT_RATE * inl[at].astype(F32) * (1.0 - here)
            dst[0, at] = here + TIME_STEP * change

    def top_add(s, dst, c):
        dst[depth - 1, cut(c)] = dst[depth - 1, cut(c)] + TIME_STEP * ghost_above(s, c)

    def bottom_add(s, dst):
        for r in strips:
            at = pl.ds(r, STRIP)
            ghost = jnp.where(has_below, gbelow[at], 0.0)
            dst[0, at] = dst[0, at] + TIME_STEP * ((1.0 + vel[0, at]) * ghost)

    def prepare_down():
        x_load.wait()
        y_load.wait()
        for k in range(kk):
            xt_cat[pl.ds(k * cx, cx)] = left_cat(xw[k].T)
            y_cat[k] = right_cat(yw[k])

    def prepare_up():
        for k in range(kk):
            x_cat[k] = left_cat(xw[k])
            yt_cat[pl.ds(3 * k * cy, 3 * cy)] = right_cat(yw[k].T)

    def project_down(plane):
        field = right_cat(plane)
        for k in range(kk):
            half = left_cat(dot(xt_cat[pl.ds(k * cx, cx)], field))
            pieces[k] = dot(half, y_cat[k])

    size_of = [1] + [1 << (nb - axis) for axis in range(nb)]

    def slot_tile(bits):
        there = tile
        for bit, size in zip(bits, size_of):
            if bit:
                there = there + size * (1 - 2 * ((tile // size) % 2))
        return there

    all_slots = [[slot % 2] + [(slot >> (nb - axis)) % 2 for axis in range(nb)] for slot in range(tiles)]
    listed = [sources_ref[0, 0, k] for k in range(kk)]
    wanted = [[listed[k] == slot_tile(bits) for k in range(kk)] for bits in all_slots]

    def fill(s, c):
        for r in range(0, rows, STRIP):
            at = pl.ds(c * rows + r, STRIP)
            values = [pieces[k, at] for k in range(kk)]
            for slot, bits in enumerate(all_slots):
                total = values[0] if slot == tiles // 2 else None
                for k in range(1, kk):
                    term = jnp.where(wanted[slot][k], values[k], 0.0)
                    total = term if total is None else total + term
                acc[(s,) + tuple(bits) + (at,)] = total

    def project_up(s):
        for k in range(kk):
            at = tuple((listed[k] // size + tile // size) % 2 for size in size_of)
            half = dot(x_cat[k], right_cat(tops[s][at]))
            halves[:, pl.ds(3 * k * cy, 3 * cy)] = left_cat(half)
        gbelow[...] = dot(halves[...], yt_cat[...])

    def put(z0, n, i):
        return pltpu.make_async_copy(f2.at[pl.ds(z0, n)], out.at[pl.ds(z0, n)], out_sems.at[i])

    chunks = range(CHUNKS)

    def reduce_enter(s):
        for c in chunks:
            fill(s, c)
            reduce_core(s, c).start()

    def reduce_cores(s):
        for c in chunks:
            add_core(s, c)
            reduce_stage(s, c, 0).start()

    def reduce_next(s, stage):
        for c in chunks:
            add_stage(s, c, stage)
            if stage == nb - 1:
                if_below(sum_down, s, c, "start")
            else:
                reduce_stage(s, c, stage + 1).start()

    def spread_enter(s):
        for c in chunks:
            top_arrived(s, c)
            spread(s, c, 0).start()

    def spread_next(s, stage):
        for c in chunks:
            spread(s, c, stage).wait_recv()
            if stage < nb:
                spread(s, c, stage + 1).start()

    prepare_down()
    bottom_load.wait()
    project_down(f0[0])
    reduce_enter(0)
    hs[...] = jnp.zeros_like(hs)
    f_load.wait()
    halo_send(f0, ALL, 0, depth)
    reduce_cores(0)
    spread_enter(0)
    prepare_up()
    v_load.wait()
    i_load.wait()
    halo_receive(ALL)
    top_part(f0, f1, ALL)
    for stage in range(nb):
        reduce_next(0, stage)
        spread_next(0, stage)
        if stage == 0:
            bottom_part(f0, f1, ALL)
            inner(f0, f1, ALL, 1, 3)
    inner(f0, f1, ALL, 3, 7)

    for c in chunks:
        top_add(0, f1, c)
        if_above(top_up, 1, c, "start")
        inner(f0, f1, ALL, 7 + 2 * c, 9 + 2 * c)
    spread_next(0, nb)
    project_up(0)
    bottom_add(0, f1)
    spread_enter(1)
    project_down(f1[0])
    reduce_enter(1)
    halo_send(f1, INNER, 1, depth - 1)
    halo_send(f1, TOP, depth - 1, depth)
    halo_send(f1, BOTTOM, 0, 1)
    reduce_cores(1)
    spread_next(1, 0)
    halo_receive(INNER)
    inner(f1, f2, INNER, 1, 3)
    for stage in range(nb):
        reduce_next(1, stage)
        spread_next(1, stage + 1)
        if stage == 0:
            halo_receive(BOTTOM)
            bottom_part(f1, f2, BOTTOM)
            halo_receive(TOP)
            top_part(f1, f2, TOP)
            inner(f1, f2, INNER, 3, 6)
    project_up(1)
    bottom_add(1, f2)
    inner(f1, f2, INNER, 6, 8)
    put(0, 8, 0).start()
    inner(f1, f2, INNER, 8, depth - 1)
    put(8, depth - 9, 1).start()
    for c in chunks:
        top_add(1, f2, c)
    put(depth - 1, 1, 2).start()

    for s in range(STEPS):
        for c in range(CHUNKS):
            if_above(top_up, s, c, "wait_send")
            if_below(sum_down, s, c, "wait_send")
            reduce_core(s, c).wait_send()
            for stage in range(nb):
                reduce_stage(s, c, stage).wait_send()
            for stage in range(nb + 1):
                spread(s, c, stage).wait_send()
    for g in range(4):
        for d in range(4):
            halo_copy(g, d).wait_send()
    put(0, 8, 0).wait()
    put(8, depth - 9, 1).wait()
    put(depth - 1, 1, 2).wait()


def on_device(tiles, lifts, oxygen, velocity, spacing, inlets, proj_x, proj_y, sources):
    nb = tiles.bit_length() - 2
    field = oxygen[0, :, 0]
    speed = velocity[0, :, 0]
    depth, cx, cy = field.shape
    kk = proj_x.shape[2]
    two = (2,) * nb
    any_spec = pl.BlockSpec(memory_space=pl.ANY)
    smem = pl.BlockSpec(memory_space=pltpu.SMEM)
    plane = (cx, cy)
    dma = pltpu.SemaphoreType.DMA
    result = pl.pallas_call(
        functools.partial(kernel, tiles, lifts, nb),
        out_shape=jax.ShapeDtypeStruct(field.shape, F32),
        in_specs=[smem, smem] + [any_spec] * 5,
        out_specs=any_spec,
        scratch_shapes=[
            pltpu.VMEM(field.shape, F32),
            pltpu.VMEM(field.shape, F32),
            pltpu.VMEM(field.shape, F32),
            pltpu.VMEM(field.shape, F32),
            pltpu.VMEM(plane, jnp.int32),
            pltpu.VMEM((kk,) + plane, F32),
            pltpu.VMEM((kk,) + plane, F32),
        ]
        + [
            pltpu.VMEM((kk, cx, 3 * cx), BF16),
            pltpu.VMEM((kk * cx, 3 * cx), BF16),
            pltpu.VMEM((kk, 3 * cy, cy), BF16),
            pltpu.VMEM((3 * kk * cy, cy), BF16),
            pltpu.VMEM((cx, 3 * kk * cy), BF16),
            pltpu.VMEM((kk,) + plane, F32),
            pltpu.VMEM((2,) + two + plane, F32),
            pltpu.VMEM((2,) + two + plane, F32),
            pltpu.VMEM((STEPS, 2) + two + plane, F32),
            pltpu.VMEM((STEPS,) + two + plane, F32),
            pltpu.VMEM((STEPS,) + plane, F32),
            pltpu.VMEM((STEPS,) + plane, F32),
            pltpu.VMEM(plane, F32),
            pltpu.VMEM((4, 4, depth, cx), F32),
            pltpu.VMEM((4, 4, depth, cx), F32),
            pltpu.VMEM((2, cx, LANES), F32),
            dma((6,)),
            dma((3,)),
            dma((4, 4)),
            dma((4, 4)),
            dma((STEPS, nb + 1, CHUNKS)),
            dma((STEPS, nb + 1, CHUNKS)),
            dma((STEPS, nb + 1, CHUNKS)),
            dma((STEPS, nb + 1, CHUNKS)),
            dma((STEPS, 2, CHUNKS)),
            dma((STEPS, 2, CHUNKS)),
            pltpu.VMEM((4, 2, cx, LANES), F32),
        ]
        + [pltpu.VMEM((STEPS,) + (2,) * (nb - 1 - stage) + plane, F32) for stage in range(nb)],
        compiler_params=pltpu.CompilerParams(
            collective_id=0, has_side_effects=True, vmem_limit_bytes=60 * 1024 * 1024
        ),
        cost_estimate=pl.CostEstimate(flops=10**9, bytes_accessed=16 * 1024 * 1024, transcendentals=0),
    )(sources, spacing, field, speed, inlets[0, 0], proj_x[0, 0], proj_y[0, 0])
    return result[None, :, None]


def solution(mesh):
    return jax.shard_map(
        functools.partial(on_device, mesh.shape["tile"], mesh.shape["lift"]),
        mesh=mesh,
        in_specs=(
            P("lift", None, "tile", None, None),
            P("lift", None, "tile", None, None),
            P("lift"),
            P("lift", "tile", None, None),
            P("lift", "tile", None, None, None),
            P("lift", "tile", None, None, None),
            P("lift", "tile", None),
        ),
        out_specs=P("lift", None, "tile", None, None),
        check_vma=False,
    )
```

```python
import functools

import jax
import jax.numpy as jnp
from jax import lax
from jax.experimental import pallas as pl
from jax.experimental.pallas import tpu as pltpu
from jax.sharding import PartitionSpec as P

TCOL = 4
STEPS = 2
TIME_STEP = 0.1
INJECT_RATE = 2.0
AMBIENT = 1.0
MESH = pl.DeviceIdType.MESH
CHUNKS = 4
STRIP = 32
LANES = 128
ALL, INNER, TOP, BOTTOM = 0, 1, 2, 3
F32 = jnp.float32
BF16 = jnp.bfloat16


def split(value):
    high = value.astype(BF16)
    return high, (value - high.astype(F32)).astype(BF16)


def left_cat(value):
    high, low = split(value)
    return jnp.concatenate([high, low, high], axis=1)


def right_cat(value):
    high, low = split(value)
    return jnp.concatenate([high, high, low], axis=0)


def dot(left, right):
    return jnp.dot(left, right, preferred_element_type=F32)


def kernel(
    tiles, lifts, nb,
    sources_ref, spacing_ref, oxygen, velocity, inlets, proj_x, proj_y, out,
    f0, f1, f2, vel, inl, xw, yw,
    x_cat, xt_cat, y_cat, yt_cat, halves, pieces,
    tops_0, tops_1, acc, core_in, above_in, send_down, gbelow,
    hs, hr, hcol,
    load_sems, out_sems, halo_ss, halo_rs,
    ag_ss, ag_rs, rs_ss, rs_rs, z_ss, z_rs, hcol_in, *stage_in
):
    depth, cx, cy = f0.shape
    kk = xw.shape[0]
    rows = cx // CHUNKS
    tops = (tops_0, tops_1)
    tile = lax.axis_index("tile")
    lift = lax.axis_index("lift")
    column = tile % TCOL
    base = tile - column
    row_down = (tile + TCOL) % tiles
    row_up = (tile + tiles - TCOL) % tiles
    col_right = base + (column + 1) % TCOL
    col_left = base + (column + TCOL - 1) % TCOL
    has_above = lift < lifts - 1
    has_below = lift > 0

    def flipped(bit):
        size = 1 << bit
        return tile + size * (1 - 2 * ((tile // size) % 2))

    partner_core = flipped(0)
    partner = [flipped(nb - axis) for axis in range(nb)]

    bottom_load = pltpu.make_async_copy(oxygen.at[0], f0.at[0], load_sems.at[0])
    x_load = pltpu.make_async_copy(proj_x, xw, load_sems.at[1])
    y_load = pltpu.make_async_copy(proj_y, yw, load_sems.at[2])
    f_load = pltpu.make_async_copy(oxygen.at[pl.ds(1, depth - 1)], f0.at[pl.ds(1, depth - 1)], load_sems.at[3])
    v_load = pltpu.make_async_copy(velocity, vel, load_sems.at[4])
    i_load = pltpu.make_async_copy(inlets, inl, load_sems.at[5])
    for load in (bottom_load, x_load, y_load, f_load, v_load, i_load):
        load.start()

    barrier = pltpu.get_barrier_semaphore()
    peers = [partner_core] + partner + [row_down, row_up, col_right, col_left]
    for peer in peers:
        pl.semaphore_signal(barrier, inc=1, device_id={"tile": peer}, device_id_type=MESH)

    @pl.when(has_above)
    def _():
        pl.semaphore_signal(barrier, inc=1, device_id={"lift": lift + 1}, device_id_type=MESH)

    @pl.when(has_below)
    def _():
        pl.semaphore_signal(barrier, inc=1, device_id={"lift": lift - 1}, device_id_type=MESH)

    pl.semaphore_wait(barrier, len(peers) + has_above.astype(jnp.int32) + has_below.astype(jnp.int32))

    def cut(c):
        return pl.ds(c * rows, rows)

    def order(c):
        axes = list(range(nb))
        return axes if c % 2 == 0 else axes[::-1]

    def remote(src, dst, ss, rs, **where):
        return pltpu.make_async_remote_copy(
            src_ref=src, dst_ref=dst, send_sem=ss, recv_sem=rs, device_id=where, device_id_type=MESH
        )

    def top_up(s, c):
        field = oxygen if s == 0 else f1
        return remote(
            field.at[depth - 1, cut(c)],
            tops[s].at[(0,) + (0,) * nb + (cut(c),)],
            z_ss.at[s, 0, c], z_rs.at[s, 0, c], lift=lift + 1,
        )

    def spread(s, c, stage):
        if stage == nb:
            every = (slice(None),) * nb
            return remote(
                tops[s].at[(0,) + every + (cut(c),)], tops[s].at[(1,) + every + (cut(c),)],
                ag_ss.at[s, stage, c], ag_rs.at[s, stage, c], tile=partner_core,
            )
        axes = order(c)
        index = [0] * nb
        for axis in axes[:stage]:
            index[axis] = slice(None)
        there = list(index)
        there[axes[stage]] = 1
        return remote(
            tops[s].at[(0,) + tuple(index) + (cut(c),)], tops[s].at[(0,) + tuple(there) + (cut(c),)],
            ag_ss.at[s, stage, c], ag_rs.at[s, stage, c], tile=partner[axes[stage]],
        )

    def top_arrived(s, c):
        @pl.when(has_below)
        def _():
            top_up(s, c).wait_recv()

        @pl.when(lift == 0)
        def _():
            tops[s][(0,) + (0,) * nb + (cut(c),)] = jnp.zeros((rows, cy), F32)

    def reduce_core(s, c):
        every = (slice(None),) * nb
        return remote(
            acc.at[(s, 1) + every + (cut(c),)], core_in.at[(s,) + every + (cut(c),)],
            rs_ss.at[s, nb, c], rs_rs.at[s, nb, c], tile=partner_core,
        )

    def left_index(c, stage):
        axes = order(c)
        index = [slice(None)] * nb
        for axis in axes[:stage]:
            index[axis] = 0
        return index

    def reduce_stage(s, c, stage):
        axis = order(c)[stage]
        index = left_index(c, stage)
        index[axis] = 1
        every = (slice(None),) * (nb - 1 - stage)
        return remote(
            acc.at[(s, 0) + tuple(index) + (cut(c),)], stage_in[stage].at[(s,) + every + (cut(c),)],
            rs_ss.at[s, stage, c], rs_rs.at[s, stage, c], tile=partner[axis],
        )

    def add_core(s, c):
        reduce_core(s, c).wait_recv()
        every = (slice(None),) * nb
        at = (s, 0) + every + (cut(c),)
        acc[at] = acc[at] + core_in[(s,) + every + (cut(c),)]

    def add_stage(s, c, stage):
        reduce_stage(s, c, stage).wait_recv()
        index = tuple(left_index(c, stage + 1))
        at = (s, 0) + index + (cut(c),)
        every = (slice(None),) * (nb - 1 - stage)
        total = acc[at] + stage_in[stage][(s,) + every + (cut(c),)]
        if stage == nb - 1:
            send_down[s, cut(c)] = total
        else:
            acc[at] = total

    def sum_down(s, c):
        return remote(
            send_down.at[s, cut(c)], above_in.at[s, cut(c)],
            z_ss.at[s, 1, c], z_rs.at[s, 1, c], lift=lift - 1,
        )

    def ghost_above(s, c):
        @pl.when(has_above)
        def _():
            sum_down(s, c).wait_recv()

        @pl.when(lift == lifts - 1)
        def _():
            above_in[s, cut(c)] = jnp.full((rows, cy), AMBIENT, F32)

        return above_in[s, cut(c)]

    def if_below(copy_of, s, c, action):
        @pl.when(has_below)
        def _():
            getattr(copy_of(s, c), action)()

    def if_above(copy_of, s, c, action):
        @pl.when(has_above)
        def _():
            getattr(copy_of(s, c), action)()

    for c in range(CHUNKS):
        if_above(top_up, 0, c, "start")

    lane = lax.broadcasted_iota(jnp.int32, (STRIP, LANES), 1)
    halo_to = [row_down, row_up, col_right, col_left]

    def halo_copy(g, d):
        return remote(hs.at[g, d], hr.at[g, d], halo_ss.at[g, d], halo_rs.at[g, d], tile=halo_to[d])

    def halo_send(src, g, first, end):
        for z in range(first, end):
            hs[g, 0, z:z + 1, :] = src[z, cx - 1:cx, :]
            hs[g, 1, z:z + 1, :] = src[z, 0:1, :]

        def one(i, carry):
            at = pl.ds(pl.multiple_of(i * STRIP, STRIP), STRIP)
            right = jnp.zeros((STRIP, LANES), F32)
            left = jnp.zeros((STRIP, LANES), F32)
            for z in range(first, end):
                right = jnp.where(lane == z, pltpu.roll(src[z, at, cy - LANES:], (z + 1) % LANES, 1), right)
                rim = src[z, at, :LANES]
                left = jnp.where(lane == z, pltpu.roll(rim, z, 1) if z else rim, left)
            hcol[0, at] = right
            hcol[1, at] = left
            return carry

        lax.fori_loop(0, cx // STRIP, one, 0)
        hs[g, 2] = hcol[0].T[:depth]
        hs[g, 3] = hcol[1].T[:depth]
        for d in range(4):
            halo_copy(g, d).start()

    at_edge = [base == 0, base == tiles - TCOL, column == 0, column == TCOL - 1]

    def halo_receive(g):
        for d in range(4):
            halo_copy(g, d).wait_recv()
        for d in range(2):
            hr[g, d] = jnp.where(at_edge[d], 0.0, hr[g, d])
        for d in (2, 3):
            value = jnp.where(at_edge[d], 0.0, hr[g, d])
            padded = jnp.concatenate([value, jnp.zeros((LANES - depth, cx), F32)], axis=0)
            hcol_in[g, d - 2] = padded.T


    inverse = 1.0 / (spacing_ref[0] * spacing_ref[0])
    row_at = lax.broadcasted_iota(jnp.int32, (STRIP, cy), 0)
    strips = range(0, cx, STRIP)

    def stencil(src, z, g, r, under, over):
        at = pl.ds(r, STRIP)
        here = src[z, at]
        before = hr[g, 0, pl.ds(z, 1), :] if r == 0 else src[z, pl.ds(r - 1, 1), :]
        after = hr[g, 1, pl.ds(z, 1), :] if r == cx - STRIP else src[z, pl.ds(r + STRIP, 1), :]
        north = jnp.where(row_at == 0, before, pltpu.roll(here, 1, 0))
        south = jnp.where(row_at == STRIP - 1, after, pltpu.roll(here, STRIP - 1, 0))
        west = pltpu.roll(here, 1, 1)
        east = pltpu.roll(here, cy - 1, 1)
        west_rim = pltpu.roll(hcol_in[g, 0, at], (LANES - z) % LANES, 1)
        east_rim = pltpu.roll(hcol_in[g, 1, at], LANES - 1 - z, 1)
        west = jnp.concatenate([jnp.where(lane == 0, west_rim, west[:, :LANES]), west[:, LANES:]], axis=1)
        east = jnp.concatenate(
            [east[:, : cy - LANES], jnp.where(lane == LANES - 1, east_rim, east[:, cy - LANES:])], axis=1
        )
        change = (north + south + west + east - 4.0 * here) * inverse - 2.0 * here
        speed = vel[z, at]
        if under is None:
            change = change - speed * here
        else:
            below = src[under, at]
            change = change + below - speed * (here - below)
        if over is not None:
            change = change + src[over, at]
        return here, change

    def inner(src, dst, g, first, end):
        def one(z, carry):
            for r in strips:
                here, change = stencil(src, z, g, r, z - 1, z + 1)
                dst[z, pl.ds(r, STRIP)] = here + TIME_STEP * change
            return carry

        lax.fori_loop(first, end, one, 0)

    def top_part(src, dst, g):
        for r in strips:
            here, change = stencil(src, depth - 1, g, r, depth - 2, None)
            dst[depth - 1, pl.ds(r, STRIP)] = here + TIME_STEP * change

    def bottom_part(src, dst, g):
        for r in strips:
            at = pl.ds(r, STRIP)
            here, change = stencil(src, 0, g, r, None, 1)
            change = change + INJECT_RATE * inl[at].astype(F32) * (1.0 - here)
            dst[0, at] = here + TIME_STEP * change

    def top_add(s, dst, c):
        dst[depth - 1, cut(c)] = dst[depth - 1, cut(c)] + TIME_STEP * ghost_above(s, c)

    def bottom_add(s, dst):
        for r in strips:
            at = pl.ds(r, STRIP)
            ghost = jnp.where(has_below, gbelow[at], 0.0)
            dst[0, at] = dst[0, at] + TIME_STEP * ((1.0 + vel[0, at]) * ghost)

    def prepare_down():
        x_load.wait()
        y_load.wait()
        for k in range(kk):
            xt_cat[pl.ds(k * cx, cx)] = left_cat(xw[k].T)
            y_cat[k] = right_cat(yw[k])

    def prepare_up():
        for k in range(kk):
            x_cat[k] = left_cat(xw[k])
            yt_cat[pl.ds(3 * k * cy, 3 * cy)] = right_cat(yw[k].T)

    def project_down(plane):
        field = right_cat(plane)
        for k in range(kk):
            half = left_cat(dot(xt_cat[pl.ds(k * cx, cx)], field))
            pieces[k] = dot(half, y_cat[k])

    size_of = [1] + [1 << (nb - axis) for axis in range(nb)]

    def slot_tile(bits):
        there = tile
        for bit, size in zip(bits, size_of):
            if bit:
                there = there + size * (1 - 2 * ((tile // size) % 2))
        return there

    all_slots = [[slot % 2] + [(slot >> (nb - axis)) % 2 for axis in range(nb)] for slot in range(tiles)]
    listed = [sources_ref[0, 0, k] for k in range(kk)]
    wanted = [[listed[k] == slot_tile(bits) for k in range(kk)] for bits in all_slots]

    def fill(s, c):
        for r in range(0, rows, STRIP):
            at = pl.ds(c * rows + r, STRIP)
            values = [pieces[k, at] for k in range(kk)]
            for slot, bits in enumerate(all_slots):
                total = values[0] if slot == tiles // 2 else None
                for k in range(1, kk):
                    term = jnp.where(wanted[slot][k], values[k], 0.0)
                    total = term if total is None else total + term
                acc[(s,) + tuple(bits) + (at,)] = total

    def project_up(s):
        for k in range(kk):
            at = tuple((listed[k] // size + tile // size) % 2 for size in size_of)
            half = dot(x_cat[k], right_cat(tops[s][at]))
            halves[:, pl.ds(3 * k * cy, 3 * cy)] = left_cat(half)
        gbelow[...] = dot(halves[...], yt_cat[...])

    def put(z0, n, i):
        return pltpu.make_async_copy(f2.at[pl.ds(z0, n)], out.at[pl.ds(z0, n)], out_sems.at[i])

    chunks = range(CHUNKS)

    def reduce_enter(s):
        for c in chunks:
            fill(s, c)
            reduce_core(s, c).start()

    def reduce_cores(s):
        for c in chunks:
            add_core(s, c)
            reduce_stage(s, c, 0).start()

    def reduce_next(s, stage):
        for c in chunks:
            add_stage(s, c, stage)
            if stage == nb - 1:
                if_below(sum_down, s, c, "start")
            else:
                reduce_stage(s, c, stage + 1).start()

    def spread_enter(s):
        for c in chunks:
            top_arrived(s, c)
            spread(s, c, 0).start()

    def spread_next(s, stage):
        for c in chunks:
            spread(s, c, stage).wait_recv()
            if stage < nb:
                spread(s, c, stage + 1).start()

    prepare_down()
    bottom_load.wait()
    project_down(f0[0])
    reduce_enter(0)
    hs[...] = jnp.zeros_like(hs)
    f_load.wait()
    halo_send(f0, ALL, 0, depth)
    reduce_cores(0)
    prepare_up()
    v_load.wait()
    i_load.wait()
    halo_receive(ALL)
    top_part(f0, f1, ALL)
    for stage in range(nb - 1):
        reduce_next(0, stage)
    spread_enter(0)
    bottom_part(f0, f1, ALL)
    reduce_next(0, nb - 1)
    inner(f0, f1, ALL, 1, 4)
    for stage in range(nb - 1):
        spread_next(0, stage)

    for c in chunks:
        top_add(0, f1, c)
        if_above(top_up, 1, c, "start")
        inner(f0, f1, ALL, 4 + c, 5 + c)
    spread_next(0, nb - 1)
    inner(f0, f1, ALL, 8, depth - 1)
    halo_send(f1, INNER, 1, depth - 1)
    halo_send(f1, TOP, depth - 1, depth)
    spread_next(0, nb)
    spread_enter(1)
    project_up(0)
    bottom_add(0, f1)
    spread_next(1, 0)
    project_down(f1[0])
    reduce_enter(1)
    for stage in range(1, nb):
        spread_next(1, stage)
    halo_send(f1, BOTTOM, 0, 1)
    reduce_cores(1)
    halo_receive(INNER)
    inner(f1, f2, INNER, 1, 4)
    for stage in range(nb - 1):
        reduce_next(1, stage)
    spread_next(1, nb)
    project_up(1)
    reduce_next(1, nb - 1)
    halo_receive(BOTTOM)
    bottom_part(f1, f2, BOTTOM)
    bottom_add(1, f2)
    inner(f1, f2, INNER, 4, 8)
    put(0, 8, 0).start()
    halo_receive(TOP)
    top_part(f1, f2, TOP)
    inner(f1, f2, INNER, 8, depth - 1)
    put(8, depth - 9, 1).start()
    for c in chunks:
        top_add(1, f2, c)
    put(depth - 1, 1, 2).start()

    for s in range(STEPS):
        for c in range(CHUNKS):
            if_above(top_up, s, c, "wait_send")
            if_below(sum_down, s, c, "wait_send")
            reduce_core(s, c).wait_send()
            for stage in range(nb):
                reduce_stage(s, c, stage).wait_send()
            for stage in range(nb + 1):
                spread(s, c, stage).wait_send()
    for g in range(4):
        for d in range(4):
            halo_copy(g, d).wait_send()
    put(0, 8, 0).wait()
    put(8, depth - 9, 1).wait()
    put(depth - 1, 1, 2).wait()


def hand_over(parts, source, target, sems):
    count = source.shape[0] // parts
    copies = [
        pltpu.make_async_copy(source.at[pl.ds(i * count, count)], target.at[pl.ds(i * count, count)], sems.at[i])
        for i in range(parts)
    ]
    for copy in copies:
        copy.start()
    for copy in copies:
        copy.wait()


def on_device(tiles, lifts, oxygen, velocity, spacing, inlets, proj_x, proj_y, sources):
    nb = tiles.bit_length() - 2
    field = oxygen[0, :, 0]
    speed = velocity[0, :, 0]
    depth, cx, cy = field.shape
    kk = proj_x.shape[2]
    two = (2,) * nb
    any_spec = pl.BlockSpec(memory_space=pl.ANY)
    smem = pl.BlockSpec(memory_space=pltpu.SMEM)
    plane = (cx, cy)
    dma = pltpu.SemaphoreType.DMA
    result = pl.pallas_call(
        functools.partial(kernel, tiles, lifts, nb),
        out_shape=jax.ShapeDtypeStruct(field.shape, F32),
        in_specs=[smem, smem] + [any_spec] * 5,
        out_specs=any_spec,
        scratch_shapes=[
            pltpu.VMEM(field.shape, F32),
            pltpu.VMEM(field.shape, F32),
            pltpu.VMEM(field.shape, F32),
            pltpu.VMEM(field.shape, F32),
            pltpu.VMEM(plane, jnp.int32),
            pltpu.VMEM((kk,) + plane, F32),
            pltpu.VMEM((kk,) + plane, F32),
        ]
        + [
            pltpu.VMEM((kk, cx, 3 * cx), BF16),
            pltpu.VMEM((kk * cx, 3 * cx), BF16),
            pltpu.VMEM((kk, 3 * cy, cy), BF16),
            pltpu.VMEM((3 * kk * cy, cy), BF16),
            pltpu.VMEM((cx, 3 * kk * cy), BF16),
            pltpu.VMEM((kk,) + plane, F32),
            pltpu.VMEM((2,) + two + plane, F32),
            pltpu.VMEM((2,) + two + plane, F32),
            pltpu.VMEM((STEPS, 2) + two + plane, F32),
            pltpu.VMEM((STEPS,) + two + plane, F32),
            pltpu.VMEM((STEPS,) + plane, F32),
            pltpu.VMEM((STEPS,) + plane, F32),
            pltpu.VMEM(plane, F32),
            pltpu.VMEM((4, 4, depth, cx), F32),
            pltpu.VMEM((4, 4, depth, cx), F32),
            pltpu.VMEM((2, cx, LANES), F32),
            dma((6,)),
            dma((3,)),
            dma((4, 4)),
            dma((4, 4)),
            dma((STEPS, nb + 1, CHUNKS)),
            dma((STEPS, nb + 1, CHUNKS)),
            dma((STEPS, nb + 1, CHUNKS)),
            dma((STEPS, nb + 1, CHUNKS)),
            dma((STEPS, 2, CHUNKS)),
            dma((STEPS, 2, CHUNKS)),
            pltpu.VMEM((4, 2, cx, LANES), F32),
        ]
        + [pltpu.VMEM((STEPS,) + (2,) * (nb - 1 - stage) + plane, F32) for stage in range(nb)],
        compiler_params=pltpu.CompilerParams(
            collective_id=0, has_side_effects=True, vmem_limit_bytes=60 * 1024 * 1024
        ),
        cost_estimate=pl.CostEstimate(flops=10**9, bytes_accessed=16 * 1024 * 1024, transcendentals=0),
    )(sources, spacing, field, speed, inlets[0, 0], proj_x[0, 0], proj_y[0, 0])
    parts = depth // 2
    result = pl.pallas_call(
        functools.partial(hand_over, parts),
        out_shape=jax.ShapeDtypeStruct(field.shape, F32),
        in_specs=[any_spec],
        out_specs=any_spec,
        scratch_shapes=[dma((parts,))],
    )(result)
    return result[None, :, None]


def solution(mesh):
    return jax.shard_map(
        functools.partial(on_device, mesh.shape["tile"], mesh.shape["lift"]),
        mesh=mesh,
        in_specs=(
            P("lift", None, "tile", None, None),
            P("lift", None, "tile", None, None),
            P("lift"),
            P("lift", "tile", None, None),
            P("lift", "tile", None, None, None),
            P("lift", "tile", None, None, None),
            P("lift", "tile", None),
        ),
        out_specs=P("lift", None, "tile", None, None),
        check_vma=False,
    )
```

```python
import functools

import jax
import jax.numpy as jnp
from jax import lax
from jax.experimental import pallas as pl
from jax.experimental.pallas import tpu as pltpu
from jax.sharding import PartitionSpec as P

TCOL = 4
STEPS = 2
TIME_STEP = 0.1
INJECT_RATE = 2.0
AMBIENT = 1.0
MESH = pl.DeviceIdType.MESH
CHUNKS = 4
STRIP = 32
LANES = 128
ALL, INNER, TOP, BOTTOM = 0, 1, 2, 3
F32 = jnp.float32
BF16 = jnp.bfloat16


def split(value):
    high = value.astype(BF16)
    return high, (value - high.astype(F32)).astype(BF16)


def left_cat(value):
    high, low = split(value)
    return jnp.concatenate([high, low, high], axis=1)


def right_cat(value):
    high, low = split(value)
    return jnp.concatenate([high, high, low], axis=0)


def dot(left, right):
    return jnp.dot(left, right, preferred_element_type=F32)


def kernel(
    tiles, lifts, nb,
    sources_ref, spacing_ref, oxygen, velocity, inlets, proj_x, proj_y, out,
    f0, f1, f2, vel, inl, xw, yw,
    x_cat, xt_cat, y_cat, yt_cat, halves, pieces,
    tops_0, tops_1, acc, core_in, above_in, send_down, gbelow,
    hs, hr, hcol,
    load_sems, out_sems, halo_ss, halo_rs,
    ag_ss, ag_rs, rs_ss, rs_rs, z_ss, z_rs, hcol_in, *stage_in
):
    depth, cx, cy = f0.shape
    kk = xw.shape[0]
    rows = cx // CHUNKS
    tops = (tops_0, tops_1)
    tile = lax.axis_index("tile")
    lift = lax.axis_index("lift")
    column = tile % TCOL
    base = tile - column
    row_down = (tile + TCOL) % tiles
    row_up = (tile + tiles - TCOL) % tiles
    col_right = base + (column + 1) % TCOL
    col_left = base + (column + TCOL - 1) % TCOL
    has_above = lift < lifts - 1
    has_below = lift > 0

    def flipped(bit):
        size = 1 << bit
        return tile + size * (1 - 2 * ((tile // size) % 2))

    partner_core = flipped(0)
    partner = [flipped(nb - axis) for axis in range(nb)]

    bottom_load = pltpu.make_async_copy(oxygen.at[0], f0.at[0], load_sems.at[0])
    x_load = pltpu.make_async_copy(proj_x, xw, load_sems.at[1])
    y_load = pltpu.make_async_copy(proj_y, yw, load_sems.at[2])
    f_load = pltpu.make_async_copy(oxygen.at[pl.ds(1, depth - 1)], f0.at[pl.ds(1, depth - 1)], load_sems.at[3])
    v_load = pltpu.make_async_copy(velocity, vel, load_sems.at[4])
    i_load = pltpu.make_async_copy(inlets, inl, load_sems.at[5])
    for load in (bottom_load, x_load, y_load, f_load, v_load, i_load):
        load.start()

    barrier = pltpu.get_barrier_semaphore()
    peers = [partner_core] + partner + [row_down, row_up, col_right, col_left]
    for peer in peers:
        pl.semaphore_signal(barrier, inc=1, device_id={"tile": peer}, device_id_type=MESH)

    @pl.when(has_above)
    def _():
        pl.semaphore_signal(barrier, inc=1, device_id={"lift": lift + 1}, device_id_type=MESH)

    @pl.when(has_below)
    def _():
        pl.semaphore_signal(barrier, inc=1, device_id={"lift": lift - 1}, device_id_type=MESH)

    pl.semaphore_wait(barrier, len(peers) + has_above.astype(jnp.int32) + has_below.astype(jnp.int32))

    def cut(c):
        return pl.ds(c * rows, rows)

    def order(c):
        axes = list(range(nb))
        return axes if c % 2 == 0 else axes[::-1]

    def remote(src, dst, ss, rs, **where):
        return pltpu.make_async_remote_copy(
            src_ref=src, dst_ref=dst, send_sem=ss, recv_sem=rs, device_id=where, device_id_type=MESH
        )

    def top_up(s, c):
        field = oxygen if s == 0 else f1
        return remote(
            field.at[depth - 1, cut(c)],
            tops[s].at[(0,) + (0,) * nb + (cut(c),)],
            z_ss.at[s, 0, c], z_rs.at[s, 0, c], lift=lift + 1,
        )

    def spread(s, c, stage):
        if stage == nb:
            every = (slice(None),) * nb
            return remote(
                tops[s].at[(0,) + every + (cut(c),)], tops[s].at[(1,) + every + (cut(c),)],
                ag_ss.at[s, stage, c], ag_rs.at[s, stage, c], tile=partner_core,
            )
        axes = order(c)
        index = [0] * nb
        for axis in axes[:stage]:
            index[axis] = slice(None)
        there = list(index)
        there[axes[stage]] = 1
        return remote(
            tops[s].at[(0,) + tuple(index) + (cut(c),)], tops[s].at[(0,) + tuple(there) + (cut(c),)],
            ag_ss.at[s, stage, c], ag_rs.at[s, stage, c], tile=partner[axes[stage]],
        )

    def top_arrived(s, c):
        @pl.when(has_below)
        def _():
            top_up(s, c).wait_recv()

        @pl.when(lift == 0)
        def _():
            tops[s][(0,) + (0,) * nb + (cut(c),)] = jnp.zeros((rows, cy), F32)

    def reduce_core(s, c):
        every = (slice(None),) * nb
        return remote(
            acc.at[(s, 1) + every + (cut(c),)], core_in.at[(s,) + every + (cut(c),)],
            rs_ss.at[s, nb, c], rs_rs.at[s, nb, c], tile=partner_core,
        )

    def left_index(c, stage):
        axes = order(c)
        index = [slice(None)] * nb
        for axis in axes[:stage]:
            index[axis] = 0
        return index

    def reduce_stage(s, c, stage):
        axis = order(c)[stage]
        index = left_index(c, stage)
        index[axis] = 1
        every = (slice(None),) * (nb - 1 - stage)
        return remote(
            acc.at[(s, 0) + tuple(index) + (cut(c),)], stage_in[stage].at[(s,) + every + (cut(c),)],
            rs_ss.at[s, stage, c], rs_rs.at[s, stage, c], tile=partner[axis],
        )

    def add_core(s, c):
        reduce_core(s, c).wait_recv()
        every = (slice(None),) * nb
        at = (s, 0) + every + (cut(c),)
        acc[at] = acc[at] + core_in[(s,) + every + (cut(c),)]

    def add_stage(s, c, stage):
        reduce_stage(s, c, stage).wait_recv()
        index = tuple(left_index(c, stage + 1))
        at = (s, 0) + index + (cut(c),)
        every = (slice(None),) * (nb - 1 - stage)
        total = acc[at] + stage_in[stage][(s,) + every + (cut(c),)]
        if stage == nb - 1:
            send_down[s, cut(c)] = total
        else:
            acc[at] = total

    def sum_down(s, c):
        return remote(
            send_down.at[s, cut(c)], above_in.at[s, cut(c)],
            z_ss.at[s, 1, c], z_rs.at[s, 1, c], lift=lift - 1,
        )

    def ghost_above(s, c):
        @pl.when(has_above)
        def _():
            sum_down(s, c).wait_recv()

        @pl.when(lift == lifts - 1)
        def _():
            above_in[s, cut(c)] = jnp.full((rows, cy), AMBIENT, F32)

        return above_in[s, cut(c)]

    def if_below(copy_of, s, c, action):
        @pl.when(has_below)
        def _():
            getattr(copy_of(s, c), action)()

    def if_above(copy_of, s, c, action):
        @pl.when(has_above)
        def _():
            getattr(copy_of(s, c), action)()

    for c in range(CHUNKS):
        if_above(top_up, 0, c, "start")

    lane = lax.broadcasted_iota(jnp.int32, (STRIP, LANES), 1)
    halo_to = [row_down, row_up, col_right, col_left]

    def halo_copy(g, d):
        return remote(hs.at[g, d], hr.at[g, d], halo_ss.at[g, d], halo_rs.at[g, d], tile=halo_to[d])

    def halo_send(src, g, first, end):
        for z in range(first, end):
            hs[g, 0, z:z + 1, :] = src[z, cx - 1:cx, :]
            hs[g, 1, z:z + 1, :] = src[z, 0:1, :]

        def one(i, carry):
            at = pl.ds(pl.multiple_of(i * STRIP, STRIP), STRIP)
            right = jnp.zeros((STRIP, LANES), F32)
            left = jnp.zeros((STRIP, LANES), F32)
            for z in range(first, end):
                right = jnp.where(lane == z, pltpu.roll(src[z, at, cy - LANES:], (z + 1) % LANES, 1), right)
                rim = src[z, at, :LANES]
                left = jnp.where(lane == z, pltpu.roll(rim, z, 1) if z else rim, left)
            hcol[0, at] = right
            hcol[1, at] = left
            return carry

        lax.fori_loop(0, cx // STRIP, one, 0)
        hs[g, 2] = hcol[0].T[:depth]
        hs[g, 3] = hcol[1].T[:depth]
        for d in range(4):
            halo_copy(g, d).start()

    at_edge = [base == 0, base == tiles - TCOL, column == 0, column == TCOL - 1]

    def halo_receive(g):
        for d in range(4):
            halo_copy(g, d).wait_recv()
        for d in range(2):
            hr[g, d] = jnp.where(at_edge[d], 0.0, hr[g, d])
        for d in (2, 3):
            value = jnp.where(at_edge[d], 0.0, hr[g, d])
            padded = jnp.concatenate([value, jnp.zeros((LANES - depth, cx), F32)], axis=0)
            hcol_in[g, d - 2] = padded.T


    inverse = 1.0 / (spacing_ref[0] * spacing_ref[0])
    row_at = lax.broadcasted_iota(jnp.int32, (STRIP, cy), 0)
    strips = range(0, cx, STRIP)

    def stencil(src, z, g, r, under, over):
        at = pl.ds(r, STRIP)
        here = src[z, at]
        before = hr[g, 0, pl.ds(z, 1), :] if r == 0 else src[z, pl.ds(r - 1, 1), :]
        after = hr[g, 1, pl.ds(z, 1), :] if r == cx - STRIP else src[z, pl.ds(r + STRIP, 1), :]
        north = jnp.where(row_at == 0, before, pltpu.roll(here, 1, 0))
        south = jnp.where(row_at == STRIP - 1, after, pltpu.roll(here, STRIP - 1, 0))
        west = pltpu.roll(here, 1, 1)
        east = pltpu.roll(here, cy - 1, 1)
        west_rim = pltpu.roll(hcol_in[g, 0, at], (LANES - z) % LANES, 1)
        east_rim = pltpu.roll(hcol_in[g, 1, at], LANES - 1 - z, 1)
        west = jnp.concatenate([jnp.where(lane == 0, west_rim, west[:, :LANES]), west[:, LANES:]], axis=1)
        east = jnp.concatenate(
            [east[:, : cy - LANES], jnp.where(lane == LANES - 1, east_rim, east[:, cy - LANES:])], axis=1
        )
        change = (north + south + west + east - 4.0 * here) * inverse - 2.0 * here
        speed = vel[z, at]
        if under is None:
            change = change - speed * here
        else:
            below = src[under, at]
            change = change + below - speed * (here - below)
        if over is not None:
            change = change + src[over, at]
        return here, change

    def inner(src, dst, g, first, end):
        def one(z, carry):
            for r in strips:
                here, change = stencil(src, z, g, r, z - 1, z + 1)
                dst[z, pl.ds(r, STRIP)] = here + TIME_STEP * change
            return carry

        lax.fori_loop(first, end, one, 0)

    def top_part(src, dst, g):
        for r in strips:
            here, change = stencil(src, depth - 1, g, r, depth - 2, None)
            dst[depth - 1, pl.ds(r, STRIP)] = here + TIME_STEP * change

    def bottom_part(src, dst, g):
        for r in strips:
            at = pl.ds(r, STRIP)
            here, change = stencil(src, 0, g, r, None, 1)
            change = change + INJECT_RATE * inl[at].astype(F32) * (1.0 - here)
            dst[0, at] = here + TIME_STEP * change

    def top_add(s, dst, c):
        dst[depth - 1, cut(c)] = dst[depth - 1, cut(c)] + TIME_STEP * ghost_above(s, c)

    def bottom_add(s, dst):
        for r in strips:
            at = pl.ds(r, STRIP)
            ghost = jnp.where(has_below, gbelow[at], 0.0)
            dst[0, at] = dst[0, at] + TIME_STEP * ((1.0 + vel[0, at]) * ghost)

    def prepare_down():
        x_load.wait()
        y_load.wait()
        for k in range(kk):
            xt_cat[pl.ds(k * cx, cx)] = left_cat(xw[k].T)
            y_cat[k] = right_cat(yw[k])

    def prepare_up():
        for k in range(kk):
            x_cat[k] = left_cat(xw[k])
            yt_cat[pl.ds(3 * k * cy, 3 * cy)] = right_cat(yw[k].T)

    def project_down(plane):
        field = right_cat(plane)
        for k in range(kk):
            half = left_cat(dot(xt_cat[pl.ds(k * cx, cx)], field))
            pieces[k] = dot(half, y_cat[k])

    size_of = [1] + [1 << (nb - axis) for axis in range(nb)]

    def slot_tile(bits):
        there = tile
        for bit, size in zip(bits, size_of):
            if bit:
                there = there + size * (1 - 2 * ((tile // size) % 2))
        return there

    all_slots = [[slot % 2] + [(slot >> (nb - axis)) % 2 for axis in range(nb)] for slot in range(tiles)]
    listed = [sources_ref[0, 0, k] for k in range(kk)]
    wanted = [[listed[k] == slot_tile(bits) for k in range(kk)] for bits in all_slots]

    def fill(s, c):
        for r in range(0, rows, STRIP):
            at = pl.ds(c * rows + r, STRIP)
            values = [pieces[k, at] for k in range(kk)]
            for slot, bits in enumerate(all_slots):
                total = values[0] if slot == tiles // 2 else None
                for k in range(1, kk):
                    term = jnp.where(wanted[slot][k], values[k], 0.0)
                    total = term if total is None else total + term
                acc[(s,) + tuple(bits) + (at,)] = total

    def project_up(s):
        for k in range(kk):
            at = tuple((listed[k] // size + tile // size) % 2 for size in size_of)
            half = dot(x_cat[k], right_cat(tops[s][at]))
            halves[:, pl.ds(3 * k * cy, 3 * cy)] = left_cat(half)
        gbelow[...] = dot(halves[...], yt_cat[...])

    def put(z0, n, i):
        return pltpu.make_async_copy(f2.at[pl.ds(z0, n)], out.at[pl.ds(z0, n)], out_sems.at[i])

    chunks = range(CHUNKS)

    def reduce_enter(s):
        for c in chunks:
            fill(s, c)
            reduce_core(s, c).start()

    def reduce_cores(s):
        for c in chunks:
            add_core(s, c)
            reduce_stage(s, c, 0).start()

    def reduce_next(s, stage):
        for c in chunks:
            add_stage(s, c, stage)
            if stage == nb - 1:
                if_below(sum_down, s, c, "start")
            else:
                reduce_stage(s, c, stage + 1).start()

    def spread_enter(s):
        for c in chunks:
            top_arrived(s, c)
            spread(s, c, 0).start()

    def spread_next(s, stage):
        for c in chunks:
            spread(s, c, stage).wait_recv()
            if stage < nb:
                spread(s, c, stage + 1).start()

    prepare_down()
    bottom_load.wait()
    project_down(f0[0])
    reduce_enter(0)
    hs[...] = jnp.zeros_like(hs)
    f_load.wait()
    halo_send(f0, ALL, 0, depth)
    reduce_cores(0)
    prepare_up()
    v_load.wait()
    i_load.wait()
    halo_receive(ALL)
    top_part(f0, f1, ALL)
    for stage in range(nb - 1):
        reduce_next(0, stage)
    spread_enter(0)
    bottom_part(f0, f1, ALL)
    reduce_next(0, nb - 1)
    inner(f0, f1, ALL, 1, 4)
    for stage in range(nb - 1):
        spread_next(0, stage)

    for c in chunks:
        top_add(0, f1, c)
        if_above(top_up, 1, c, "start")
        inner(f0, f1, ALL, 4 + c, 5 + c)
    spread_next(0, nb - 1)
    inner(f0, f1, ALL, 8, depth - 1)
    halo_send(f1, INNER, 1, depth - 1)
    halo_send(f1, TOP, depth - 1, depth)
    spread_next(0, nb)
    spread_enter(1)
    project_up(0)
    bottom_add(0, f1)
    spread_next(1, 0)
    project_down(f1[0])
    reduce_enter(1)
    for stage in range(1, nb):
        spread_next(1, stage)
    halo_send(f1, BOTTOM, 0, 1)
    reduce_cores(1)
    halo_receive(INNER)
    inner(f1, f2, INNER, 1, 4)
    for stage in range(nb - 1):
        reduce_next(1, stage)
    spread_next(1, nb)
    project_up(1)
    reduce_next(1, nb - 1)
    halo_receive(BOTTOM)
    bottom_part(f1, f2, BOTTOM)
    bottom_add(1, f2)
    inner(f1, f2, INNER, 4, 8)
    put(0, 8, 0).start()
    halo_receive(TOP)
    top_part(f1, f2, TOP)
    inner(f1, f2, INNER, 8, depth - 1)
    put(8, depth - 9, 1).start()
    for c in chunks:
        top_add(1, f2, c)
    put(depth - 1, 1, 2).start()

    for s in range(STEPS):
        for c in range(CHUNKS):
            if_above(top_up, s, c, "wait_send")
            if_below(sum_down, s, c, "wait_send")
            reduce_core(s, c).wait_send()
            for stage in range(nb):
                reduce_stage(s, c, stage).wait_send()
            for stage in range(nb + 1):
                spread(s, c, stage).wait_send()
    for g in range(4):
        for d in range(4):
            halo_copy(g, d).wait_send()
    put(0, 8, 0).wait()
    put(8, depth - 9, 1).wait()
    put(depth - 1, 1, 2).wait()


def on_device(tiles, lifts, oxygen, velocity, spacing, inlets, proj_x, proj_y, sources):
    nb = tiles.bit_length() - 2
    field = oxygen[0, :, 0]
    speed = velocity[0, :, 0]
    depth, cx, cy = field.shape
    kk = proj_x.shape[2]
    two = (2,) * nb
    any_spec = pl.BlockSpec(memory_space=pl.ANY)
    smem = pl.BlockSpec(memory_space=pltpu.SMEM)
    plane = (cx, cy)
    dma = pltpu.SemaphoreType.DMA
    result = pl.pallas_call(
        functools.partial(kernel, tiles, lifts, nb),
        out_shape=jax.ShapeDtypeStruct(field.shape, F32),
        in_specs=[smem, smem] + [any_spec] * 5,
        out_specs=any_spec,
        scratch_shapes=[
            pltpu.VMEM(field.shape, F32),
            pltpu.VMEM(field.shape, F32),
            pltpu.VMEM(field.shape, F32),
            pltpu.VMEM(field.shape, F32),
            pltpu.VMEM(plane, jnp.int32),
            pltpu.VMEM((kk,) + plane, F32),
            pltpu.VMEM((kk,) + plane, F32),
        ]
        + [
            pltpu.VMEM((kk, cx, 3 * cx), BF16),
            pltpu.VMEM((kk * cx, 3 * cx), BF16),
            pltpu.VMEM((kk, 3 * cy, cy), BF16),
            pltpu.VMEM((3 * kk * cy, cy), BF16),
            pltpu.VMEM((cx, 3 * kk * cy), BF16),
            pltpu.VMEM((kk,) + plane, F32),
            pltpu.VMEM((2,) + two + plane, F32),
            pltpu.VMEM((2,) + two + plane, F32),
            pltpu.VMEM((STEPS, 2) + two + plane, F32),
            pltpu.VMEM((STEPS,) + two + plane, F32),
            pltpu.VMEM((STEPS,) + plane, F32),
            pltpu.VMEM((STEPS,) + plane, F32),
            pltpu.VMEM(plane, F32),
            pltpu.VMEM((4, 4, depth, cx), F32),
            pltpu.VMEM((4, 4, depth, cx), F32),
            pltpu.VMEM((2, cx, LANES), F32),
            dma((6,)),
            dma((3,)),
            dma((4, 4)),
            dma((4, 4)),
            dma((STEPS, nb + 1, CHUNKS)),
            dma((STEPS, nb + 1, CHUNKS)),
            dma((STEPS, nb + 1, CHUNKS)),
            dma((STEPS, nb + 1, CHUNKS)),
            dma((STEPS, 2, CHUNKS)),
            dma((STEPS, 2, CHUNKS)),
            pltpu.VMEM((4, 2, cx, LANES), F32),
        ]
        + [pltpu.VMEM((STEPS,) + (2,) * (nb - 1 - stage) + plane, F32) for stage in range(nb)],
        compiler_params=pltpu.CompilerParams(
            collective_id=0, has_side_effects=True, vmem_limit_bytes=60 * 1024 * 1024
        ),
        cost_estimate=pl.CostEstimate(flops=10**9, bytes_accessed=16 * 1024 * 1024, transcendentals=0),
    )(sources, spacing, field, speed, inlets[0, 0], proj_x[0, 0], proj_y[0, 0])
    return result[None, :, None]


def solution(mesh):
    return jax.shard_map(
        functools.partial(on_device, mesh.shape["tile"], mesh.shape["lift"]),
        mesh=mesh,
        in_specs=(
            P("lift", None, "tile", None, None),
            P("lift", None, "tile", None, None),
            P("lift"),
            P("lift", "tile", None, None),
            P("lift", "tile", None, None, None),
            P("lift", "tile", None, None, None),
            P("lift", "tile", None),
        ),
        out_specs=P("lift", None, "tile", None, None),
        check_vma=False,
    )
```
